256 devices in a mesh: section: 32 (over z, x_hi, core), dp: 8 (over x_lo, y).
Axes of the slice: x: 4 (x_hi: 2, x_lo: 2; x = x_hi * 2 + x_lo), y: 4, z: 8, core: 2. Of those that a mesh axis runs over, the one named last changes fastest.
Arguments:
- inputs: bfloat16 [32, 1024, 6144], P('section', 'dp'), may hold values from -6 to 6
- stash: bfloat16 [32, 1024, 6144], P('section', 'dp'), may hold values from -6 to 6
- grad_in: bfloat16 [32, 1024, 6144], P('section', 'dp'), may hold values from -6 to 6
- proj: bfloat16 [32, 6144, 512], P('section', 'dp'), may hold values from -0.5 to 0.5
- gain: bfloat16 [32, 6144], P('section', 'dp'), may hold values from 0.099609375 to 1.8984375
- fwd_docs: int32 [32, 1024], P('section', 'dp'), may hold values from 0 to 63, never falling along the last dimension, each value on 1 to 64 neighbouring positions
- bwd_docs: int32 [32, 1024], P('section', 'dp'), may hold values from 0 to 63, never falling along the last dimension, each value on 1 to 64 neighbouring positions
Outputs:
- handed: bfloat16 [32, 1024, 6144], P('section', 'dp')
- returned: bfloat16 [32, 1024, 6144], P('section', 'dp')
- parked: bfloat16 [32, 1024, 6144], P('section', 'dp')
- proj_grad: bfloat16 [32, 6144, 512], P('section', 'dp')
- gain_grad: bfloat16 [32, 6144], P('section', 'dp')
The draws below stay inside these ranges and needn't reach their ends.
Inputs may be any that keep to these rules, and one draw needn't show every extreme that they name: `fwd_docs`: document ids never fall along the tokens of a micro-batch; every id is used, no document is longer than 64 tokens, and one is exactly 64 long. Attention stays inside one data group's 128 tokens. `bwd_docs`: as for fwd_docs.
All inputs are finite; a program needn't handle non-finite values.
Results may differ from the reference program's by a relative error of at most 0.027.
Values may be sent and summed in bfloat16 or wider, within the bound.
A program may use at most 128 MiB of HBM per device.

```python
import math
import jax
import jax.numpy as jnp
import numpy as np
from jax import lax

D = 6144
HD = 128
TOK_DEV = 128
TOKENS = 1024
DOCS = 64
N_SECTION = 32
N_DP = 8


def spiked(array, stream_key, source, target, parts, factor):
    def block_of(dim):
        return (jnp.arange(array.shape[dim]) // (array.shape[dim] // parts)).reshape((-1,) + (1,) * (array.ndim - 1 - dim))

    near = jax.random.permutation(stream_key, parts)[block_of(target)]
    other_side = (block_of(target) + parts // 2) % parts
    return jnp.where((block_of(source) == near) | (block_of(source) == other_side), factor * array, array)


def steps_of(own_key, shape, pieces, low, top_value):
    def one(position, blocks):
        draws = jax.random.uniform(jax.random.fold_in(jax.random.fold_in(own_key, 6), position), (blocks,), jnp.float32, low / len(pieces), top_value / len(pieces))
        return jnp.repeat(jnp.exp(draws), shape[position] // blocks).reshape((-1,) + (1,) * (len(shape) - position - 1))

    factor_of = one(*pieces[0])
    for cut in pieces[1:]:
        factor_of = factor_of * one(*cut)
    return factor_of


def profile(number_of, total, most, lean):
    weights = [(1 << 20) // math.isqrt(rank ** lean) + 1 for rank in range(2, number_of + 1)]
    rest, counts = total - most - (number_of - 1), [1] * (number_of - 1)
    while rest > 0:
        movable = [i for i in range(number_of - 1) if counts[i] < most]
        mass, left = sum([weights[i] for i in movable]), rest
        for i in movable:
            addition = min(most - counts[i], max(1, left * weights[i] // mass), rest)
            counts[i] = counts[i] + addition
            rest = rest - addition
    return np.array([most] + counts)


def ragged(stream_key, amount, total, limit, skew):
    if amount == 2:
        one = jax.random.randint(stream_key, (), max(1, total - limit), min(limit, total - 1) + 1)
        return jnp.stack([one, total - one])
    lengths = jnp.asarray(profile(amount, total, limit, skew), jnp.int32)
    couples = (amount - 1) // 2
    donor, receiver = lengths[1:1 + 2 * couples:2], lengths[2:2 + 2 * couples:2]
    room = jnp.minimum(donor - 1, limit - receiver)
    shifted = jax.random.randint(jax.random.fold_in(stream_key, 1), (couples,), 0, 1 << 20) % (room + 1)
    lengths = lengths.at[1:1 + 2 * couples:2].set(donor - shifted).at[2:2 + 2 * couples:2].set(receiver + shifted)
    return lengths[jax.random.permutation(jax.random.fold_in(stream_key, 2), amount)]


def gaussian(own_key, shape, scale, reach, cuts=(), held_as=jnp.bfloat16):
    level = steps_of(own_key, shape, cuts, -0.22, 0.18) if cuts else 1.0
    array = jax.random.normal(own_key, shape, jnp.float32) * scale * level
    return jnp.minimum(jnp.maximum(array, -reach), reach).astype(held_as)


def heavy_noise(rng, shape, spread, most, pieces, heavy, dtype=jnp.bfloat16):
    drawn = spread * jax.random.normal(rng, shape, jnp.float32)
    if pieces:
        drawn = drawn * steps_of(rng, shape, pieces, -0.22, 0.18)
    return jnp.clip(spiked(drawn, jax.random.fold_in(rng, 3), *heavy), -most, most).astype(dtype)


def setup_inputs(seed: int = 0) -> dict:
    keys = jax.random.split(jax.random.key(seed), 8)
    return {
        "inputs": gaussian(keys[0], (N_SECTION, TOKENS, D), 1.0, 6.0, ((0, 32), (1, 8))),
        "stash": heavy_noise(keys[1], (N_SECTION, TOKENS, D), 1.0, 6.0, ((0, 32), (1, 8)), (1, 2, 8, 2.0)),
        "grad_in": gaussian(keys[2], (N_SECTION, TOKENS, D), 1.0, 6.0, ((0, 32), (1, 8))),
        "proj": gaussian(keys[3], (N_SECTION, D, 4 * HD), HD ** -0.5, 0.5, ((0, 32), (1, 8))),
        "gain": jnp.clip(1.0 + 0.18 * jax.random.normal(keys[4], (N_SECTION, D), jnp.float32), 0.099609375, 1.8984375).astype(jnp.bfloat16),
        "fwd_docs": jax.vmap(lambda own: jnp.searchsorted(jnp.cumsum(ragged(own, DOCS, TOKENS, 64, 1)), jnp.arange(TOKENS), side="right"))(jax.random.split(keys[5], N_SECTION)).reshape((N_SECTION, TOKENS)).astype(jnp.int32),
        "bwd_docs": jax.vmap(lambda own: jnp.searchsorted(jnp.cumsum(ragged(own, DOCS, TOKENS, 64, 1)), jnp.arange(TOKENS), side="right"))(jax.random.split(keys[6], N_SECTION)).reshape((N_SECTION, TOKENS)).astype(jnp.int32),
    }


def section_layer(activations, weights, norm_gain, doc_ids):
    head_size = weights.shape[1] // 4
    tok_count = activations.shape[0]
    width = activations.shape[1]
    head_count = width // head_size
    widened = activations.astype(jnp.float32)
    average = lax.optimization_barrier(jnp.mean(widened, axis=-1, keepdims=True))
    centred = widened - average
    variance = lax.optimization_barrier(jnp.mean(centred * centred, axis=-1, keepdims=True))
    normed = (centred * lax.rsqrt(variance + 1e-05) * norm_gain.astype(jnp.float32)).astype(jnp.bfloat16)
    blocks = normed.reshape(tok_count, head_count, head_size).astype(jnp.float32)
    in_maps = weights[:, :3 * head_size].reshape(head_count, head_size, 3 * head_size).astype(jnp.float32)
    projected = jnp.einsum('thc,hce->the', blocks, in_maps)
    queries = (projected[:, :, :head_size] * head_size ** (-0.5)).astype(jnp.bfloat16)
    key_rows = projected[:, :, head_size:2 * head_size].astype(jnp.bfloat16)
    value_rows = projected[:, :, 2 * head_size:].astype(jnp.bfloat16)
    scores = jnp.einsum('thd,shd->hts', queries.astype(jnp.float32), key_rows.astype(jnp.float32))
    row_ids = lax.broadcasted_iota(jnp.int32, (tok_count, tok_count), 0)
    col_ids = lax.broadcasted_iota(jnp.int32, (tok_count, tok_count), 1)
    allowed = (col_ids <= row_ids) & (doc_ids[:, None] == doc_ids[None, :])
    exp_scores = jnp.where(allowed[None], jnp.exp(scores), jnp.float32(0.0))
    attn_probs = (exp_scores / lax.optimization_barrier(jnp.sum(exp_scores, axis=-1, keepdims=True))).astype(jnp.bfloat16)
    attended = jnp.einsum('hts,shd->thd', attn_probs.astype(jnp.float32), value_rows.astype(jnp.float32)).astype(jnp.bfloat16)
    out_maps = weights[:, 3 * head_size:].reshape(head_count, head_size, head_size).astype(jnp.float32)
    mixed = jnp.einsum('thd,hcd->thc', attended.astype(jnp.float32), out_maps).reshape(tok_count, width)
    return (widened + mixed).astype(jnp.bfloat16)

def section_forward(operands):
    activations, weights, norm_gain, doc_ids = operands
    grouped = activations.reshape(N_DP, TOK_DEV, D)
    grouped_docs = doc_ids.reshape(N_DP, TOK_DEV)
    result = jax.vmap(section_layer, in_axes=(0, None, None, 0))(grouped, weights, norm_gain, grouped_docs)
    return result.reshape(TOKENS, D)

def section_backward(operands):
    stored, weights, norm_gain, doc_ids, incoming = operands

    def one_group(stored_rows, group_docs, cotangent):

        def local_layer(acts_in, weights_in, gain_in):
            return section_layer(acts_in, weights_in, gain_in, group_docs)
        unused, pullback = jax.vjp(local_layer, stored_rows, weights, norm_gain)
        return pullback(cotangent)
    back_acts, weight_terms, gain_terms = jax.vmap(one_group)(stored.reshape(N_DP, TOK_DEV, D), doc_ids.reshape(N_DP, TOK_DEV), incoming.reshape(N_DP, TOK_DEV, D))
    weight_grad = (lax.optimization_barrier(jnp.sum(weight_terms.astype(jnp.float32), axis=0)) / N_DP).astype(jnp.bfloat16)
    gain_grad = (lax.optimization_barrier(jnp.sum(gain_terms.astype(jnp.float32), axis=0)) / N_DP).astype(jnp.bfloat16)
    return (back_acts.reshape(TOKENS, D), weight_grad, gain_grad)

def reference(inputs, stash, grad_in, proj, gain, fwd_docs, bwd_docs):
    outputs = lax.map(section_forward, (inputs, proj, gain, fwd_docs))
    handed = jnp.roll(outputs, 1, axis=0)
    parked = inputs[::-1]
    fetched = stash[::-1]
    back_acts, proj_grad, gain_grad = lax.map(section_backward, (fetched, proj, gain, bwd_docs, grad_in))
    returned = jnp.concatenate([back_acts[1:], jnp.zeros_like(back_acts[:1])], axis=0)
    return (handed, returned, parked, proj_grad, gain_grad)
```

```python
import functools

import jax
import jax.numpy as jnp
from jax import lax
from jax.experimental import pallas as pl
from jax.experimental.pallas import tpu as pltpu
from jax.sharding import PartitionSpec as P

MESH = pl.DeviceIdType.MESH
F32 = jnp.float32
BF16 = jnp.bfloat16
NN = (((1,), (0,)), ((), ()))
NT = (((1,), (1,)), ((), ()))
TN = (((0,), (0,)), ((), ()))


def dot(a, b, dims):
    return lax.dot_general(a, b, dims, preferred_element_type=F32)


def kernel(
    n_sec,
    n_dp,
    x_hbm,
    st_hbm,
    gr_hbm,
    w_ref,
    gain_ref,
    fdoc_ref,
    bdoc_ref,
    handed,
    returned,
    parked,
    pgrad,
    ggrad,
    xv,
    sv,
    xf,
    xb,
    gb,
    fwd_out,
    bwd_out,
    dxh,
    dw,
    dg,
    zero,
    pf_own,
    pb_own,
    pf,
    pb,
    sums,
    total,
    loc_sem,
    xf_s,
    xf_r,
    xb_s,
    xb_r,
    gb_s,
    gb_r,
    pf_s,
    pf_r,
    pb_s,
    pb_r,
    ho_s,
    ho_r,
    re_s,
    re_r,
    su_s,
    su_r,
    pa_s,
    pa_r,
):
    tokens, width = x_hbm.shape
    cols = width // n_dp
    hd = w_ref.shape[1] // 4
    heads = cols // hd
    scale = hd ** (-0.5)
    s = lax.axis_index("section")
    g = lax.axis_index("dp")
    mirror = n_sec - 1 - s
    nxt = lax.rem(s + 1, n_sec)
    prv = lax.rem(s + n_sec - 1, n_sec)

    def span(j):
        return pl.ds(pl.multiple_of(j * cols, 128), cols)

    def remote(src, dst, ss, rs, dev):
        return pltpu.make_async_remote_copy(
            src_ref=src,
            dst_ref=dst,
            send_sem=ss,
            recv_sem=rs,
            device_id=dev,
            device_id_type=MESH,
        )

    def each(first, body):
        def step(k, _):
            body(lax.rem(g + k, n_dp))
            return 0

        lax.fori_loop(first, n_dp, step, 0)

    def xf_copy(j):
        return remote(x_hbm.at[:, span(j)], xf.at[g], xf_s.at[j], xf_r.at[g], (s, j))

    def gb_copy(j):
        return remote(gr_hbm.at[:, span(j)], gb.at[g], gb_s.at[j], gb_r.at[g], (s, j))

    def xb_copy(j):
        return remote(st_hbm.at[:, span(j)], xb.at[g], xb_s.at[j], xb_r.at[g], (mirror, j))

    def pf_copy(j):
        return remote(pf_own, pf.at[g], pf_s.at[j], pf_r.at[g], (s, j))

    def pb_copy(j):
        return remote(pb_own, pb.at[g], pb_s.at[j], pb_r.at[g], (mirror, j))

    def ho_copy(j):
        return remote(fwd_out.at[j], handed.at[:, span(g)], ho_s.at[j], ho_r.at[g], (nxt, j))

    def re_copy(j):
        return remote(bwd_out.at[j], returned.at[:, span(g)], re_s.at[j], re_r.at[g], (prv, j))

    def su_copy(j):
        return remote(sums.at[g], sums.at[g], su_s.at[j], su_r.at[g], (s, j))

    def pa_copy():
        return remote(x_hbm, parked, pa_s, pa_r, (mirror, g))

    def xf_in(j):
        return remote(x_hbm.at[:, span(j)], xf.at[j], xf_s.at[j], xf_r.at[j], (s, j))

    def gb_in(j):
        return remote(gr_hbm.at[:, span(j)], gb.at[j], gb_s.at[j], gb_r.at[j], (s, j))

    def xb_in(j):
        return remote(st_hbm.at[:, span(j)], xb.at[j], xb_s.at[j], xb_r.at[j], (mirror, j))

    def pf_in(j):
        return remote(pf_own, pf.at[j], pf_s.at[j], pf_r.at[j], (s, j))

    def pb_in(j):
        return remote(pb_own, pb.at[j], pb_s.at[j], pb_r.at[j], (mirror, j))

    def ho_in(j):
        return remote(fwd_out.at[j], handed.at[:, span(j)], ho_s.at[j], ho_r.at[j], (nxt, j))

    def re_in(j):
        return remote(bwd_out.at[j], returned.at[:, span(j)], re_s.at[j], re_r.at[j], (prv, j))

    def su_in(j):
        return remote(sums.at[j], sums.at[j], su_s.at[j], su_r.at[j], (s, j))

    x_load = pltpu.make_async_copy(x_hbm, xv, loc_sem.at[0])
    s_load = pltpu.make_async_copy(st_hbm, sv, loc_sem.at[1])
    xf_load = pltpu.make_async_copy(x_hbm.at[:, span(g)], xf.at[g], loc_sem.at[2])
    gb_load = pltpu.make_async_copy(gr_hbm.at[:, span(g)], gb.at[g], loc_sem.at[3])
    s_load.start()
    x_load.start()
    xf_load.start()
    gb_load.start()

    barrier = pltpu.get_barrier_semaphore()

    def greet(k, _):
        for section in (mirror, nxt, prv):
            pl.semaphore_signal(barrier, inc=1, device_id=(section, k), device_id_type=MESH)
        return 0

    lax.fori_loop(0, n_dp, greet, 0)
    each(
        1,
        lambda j: pl.semaphore_signal(barrier, inc=1, device_id=(s, j), device_id_type=MESH),
    )
    pl.semaphore_wait(barrier, 4 * n_dp - 1)

    each(0, lambda j: xb_copy(j).start())
    each(1, lambda j: xf_copy(j).start())
    each(1, lambda j: gb_copy(j).start())

    lanes = lax.broadcasted_iota(jnp.int32, (tokens, 128), 1)
    rows8 = lax.broadcasted_iota(jnp.int32, (8, 128), 0)
    chunk = 512

    def statistics(ref):
        def lane_sum(fn):
            def step(c, acc):
                part = ref[:, pl.ds(pl.multiple_of(c * chunk, chunk), chunk)].astype(F32)
                part = fn(part)
                for i in range(chunk // 128):
                    acc = acc + part[:, i * 128 : (i + 1) * 128]
                return acc

            acc = lax.fori_loop(0, width // chunk, step, jnp.zeros((tokens, 128), F32))
            return jnp.sum(acc, axis=1, keepdims=True)

        mean = lane_sum(lambda v: v) / width

        def squared(v):
            return (v - mean) * (v - mean)

        rstd = lax.rsqrt(lane_sum(squared) / width + 1e-05)
        both = jnp.where(lanes == 0, mean, jnp.where(lanes == 1, rstd, 0.0))
        return both.T[0:8, :]

    s_load.wait()
    pb_own[...] = statistics(sv)
    each(0, lambda j: pb_copy(j).start())
    x_load.wait()
    own = statistics(xv)
    own = jnp.where(rows8 == 2, jnp.broadcast_to(fdoc_ref[...].astype(F32), (8, 128)), own)
    own = jnp.where(rows8 == 3, jnp.broadcast_to(bdoc_ref[...].astype(F32), (8, 128)), own)
    pf_own[...] = own
    pf[g] = own
    each(1, lambda j: pf_copy(j).start())

    row_ids = lax.broadcasted_iota(jnp.int32, (tokens, tokens), 0)
    col_ids = lax.broadcasted_iota(jnp.int32, (tokens, tokens), 1)
    causal = col_ids <= row_ids

    def wide(row):
        return jnp.broadcast_to(row, (128, 128)).T

    def allowed_of(docs):
        across = jnp.broadcast_to(docs, (128, 128))
        return causal & (across == across.T)

    def attention(normed, h, allowed):
        w_in = w_ref[h * hd : (h + 1) * hd, : 3 * hd]
        w_out = w_ref[h * hd : (h + 1) * hd, 3 * hd :]
        projected = dot(normed, w_in, NN)
        q = (projected[:, :hd] * scale).astype(BF16)
        k = projected[:, hd : 2 * hd].astype(BF16)
        v = projected[:, 2 * hd :].astype(BF16)
        e = jnp.where(allowed, jnp.exp(dot(q, k, NT)), 0.0)
        p = e * (1.0 / jnp.sum(e, axis=-1, keepdims=True))
        p16 = p.astype(BF16)
        a = dot(p16, v, NN).astype(BF16)
        return w_in, w_out, q, k, v, p, p16, a

    xf_load.wait()
    gb_load.wait()

    def forward(k, _):
        j = lax.rem(g + n_dp - k, n_dp)

        @pl.when(k > 0)
        def _():
            pf_in(j).wait_recv()
            xf_in(j).wait_recv()

        mean = wide(pf[j, 0:1, :])
        rstd = wide(pf[j, 1:2, :])
        allowed = allowed_of(pf[j, 2:3, :])
        for h in range(heads):
            at = slice(h * hd, (h + 1) * hd)
            x = xf[j, :, at].astype(F32)
            normed = ((x - mean) * rstd * gain_ref[:, at].astype(F32)).astype(BF16)
            w_in, w_out, q, key, v, p, p16, a = attention(normed, h, allowed)
            fwd_out[j, :, at] = (x + dot(a, w_out, NT)).astype(BF16)
        ho_copy(j).start()
        return 0

    lax.fori_loop(0, n_dp, forward, 0)

    each(0, lambda j: xb_copy(j).wait_send())
    pa_copy().start()

    dw[...] = jnp.zeros_like(dw)
    dg[...] = jnp.zeros_like(dg)

    group_ids = lax.broadcasted_iota(jnp.int32, (n_dp, 128), 0)

    def backward(k, parts):
        j = lax.rem(g + n_dp - k, n_dp)

        @pl.when(k > 0)
        def _():
            gb_in(j).wait_recv()

        pb_in(j).wait_recv()
        xb_in(j).wait_recv()
        mean = wide(pb[j, 0:1, :])
        rstd = wide(pb[j, 1:2, :])
        allowed = allowed_of(pf[j, 3:4, :])
        first = jnp.zeros((tokens, hd), F32)
        second = jnp.zeros((tokens, hd), F32)
        for h in range(heads):
            at = slice(h * hd, (h + 1) * hd)
            gain = gain_ref[:, at].astype(F32)
            xhat = (xb[j, :, at].astype(F32) - mean) * rstd
            normed = (xhat * gain).astype(BF16)
            w_in, w_out, q, key, v, p, p16, a = attention(normed, h, allowed)
            dy = gb[j, :, at]
            dw[at, 3 * hd :] += dot(dy, a, TN)
            da = dot(dy, w_out, NN).astype(BF16)
            dp = dot(da, v, NT)
            dv = dot(p16, da, TN).astype(BF16)
            ds = (p * (dp - jnp.sum(dp * p, axis=-1, keepdims=True))).astype(BF16)
            dq = (dot(ds, key, NN) * scale).astype(BF16)
            dk = dot(ds, q, TN).astype(BF16)
            dproj = jnp.concatenate([dq, dk, dv], axis=1)
            dw[at, : 3 * hd] += dot(normed, dproj, TN)
            dn = dot(dproj, w_in, NT)
            dg[0:1, at] += jnp.sum(dn * xhat, axis=0, keepdims=True)
            back = dn * gain
            dxh[j, :, at] = back
            first = first + back
            second = second + back * xhat
        here = group_ids == j
        return (
            jnp.where(here, jnp.sum(first.T, axis=0, keepdims=True), parts[0]),
            jnp.where(here, jnp.sum(second.T, axis=0, keepdims=True), parts[1]),
        )

    blank = jnp.zeros((n_dp, 128), F32)
    parts = lax.fori_loop(0, n_dp, backward, (blank, blank))
    sums[g, 0] = parts[0]
    sums[g, 1] = parts[1]

    each(1, lambda j: su_copy(j).start())
    pgrad[...] = (dw[...] * (1.0 / n_dp)).astype(BF16)
    ggrad[...] = (dg[0:1, :] * (1.0 / n_dp)).astype(BF16)
    each(1, lambda j: su_in(j).wait_recv())
    acc = sums[0]
    for i in range(1, n_dp):
        acc = acc + sums[i]
    total[...] = acc * (1.0 / width)

    @pl.when(s > 0)
    def _():
        def finish(k, _):
            j = lax.rem(g + k, n_dp)
            mean = wide(pb[j, 0:1, :])
            rstd = wide(pb[j, 1:2, :])
            here = group_ids == j
            c1 = wide(jnp.sum(jnp.where(here, total[0], 0.0), axis=0, keepdims=True))
            c2 = wide(jnp.sum(jnp.where(here, total[1], 0.0), axis=0, keepdims=True))
            for h in range(heads):
                at = slice(h * hd, (h + 1) * hd)
                xhat = (xb[j, :, at].astype(F32) - mean) * rstd
                back = rstd * (dxh[j, :, at] - c1 - xhat * c2)
                bwd_out[j, :, at] = (gb[j, :, at].astype(F32) + back).astype(BF16)
            re_copy(j).start()
            return 0

        lax.fori_loop(0, n_dp, finish, 0)

    @pl.when(s == n_sec - 1)
    def _():
        zero[...] = jnp.zeros_like(zero)

        def fill(j):
            return pltpu.make_async_copy(zero, returned.at[:, span(j)], re_r.at[j])

        each(0, lambda j: fill(j).start())
        each(0, lambda j: fill(j).wait())

    each(0, lambda j: ho_in(j).wait_recv())

    @pl.when(s < n_sec - 1)
    def _():
        each(0, lambda j: re_in(j).wait_recv())

    pa_copy().wait_recv()
    each(1, lambda j: xf_copy(j).wait_send())
    each(1, lambda j: gb_copy(j).wait_send())
    each(1, lambda j: pf_copy(j).wait_send())
    each(0, lambda j: pb_copy(j).wait_send())
    each(1, lambda j: su_copy(j).wait_send())
    each(0, lambda j: ho_copy(j).wait_send())

    @pl.when(s > 0)
    def _():
        each(0, lambda j: re_copy(j).wait_send())

    pa_copy().wait_send()


def local(n_sec, n_dp, inputs, stash, grad_in, proj, gain, fwd_docs, bwd_docs):
    tokens, width = inputs.shape[1:]
    rows, four = proj.shape[1:]
    blocks = (n_dp, tokens, rows)
    row_sem = pltpu.SemaphoreType.DMA((n_dp,))
    anywhere = pl.BlockSpec(memory_space=pl.ANY)
    vmem = pl.BlockSpec(memory_space=pltpu.VMEM)
    handed, returned, parked, pgrad, ggrad = pl.pallas_call(
        functools.partial(kernel, n_sec, n_dp),
        out_shape=[jax.ShapeDtypeStruct((tokens, width), BF16)] * 3
        + [
            jax.ShapeDtypeStruct((rows, four), BF16),
            jax.ShapeDtypeStruct((1, rows), BF16),
        ],
        in_specs=[anywhere] * 3 + [vmem] * 4,
        out_specs=[anywhere] * 3 + [vmem] * 2,
        scratch_shapes=[
            pltpu.VMEM((tokens, width), BF16),
            pltpu.VMEM((tokens, width), BF16),
            pltpu.VMEM(blocks, BF16),
            pltpu.VMEM(blocks, BF16),
            pltpu.VMEM(blocks, BF16),
            pltpu.VMEM(blocks, BF16),
            pltpu.VMEM(blocks, BF16),
            pltpu.VMEM(blocks, F32),
            pltpu.VMEM((rows, four), F32),
            pltpu.VMEM((8, rows), F32),
            pltpu.VMEM((tokens, rows), BF16),
            pltpu.VMEM((8, 128), F32),
            pltpu.VMEM((8, 128), F32),
            pltpu.VMEM((n_dp, 8, 128), F32),
            pltpu.VMEM((n_dp, 8, 128), F32),
            pltpu.VMEM((n_dp, 2, n_dp, 128), F32),
            pltpu.VMEM((2, n_dp, 128), F32),
            pltpu.SemaphoreType.DMA((4,)),
        ]
        + [row_sem] * 16
        + [pltpu.SemaphoreType.DMA, pltpu.SemaphoreType.DMA],
        compiler_params=pltpu.CompilerParams(
            collective_id=0, has_side_effects=True, vmem_limit_bytes=48 * 1024 * 1024
        ),
    )(inputs[0], stash[0], grad_in[0], proj[0], gain, fwd_docs, bwd_docs)
    return handed[None], returned[None], parked[None], pgrad[None], ggrad


def solution(mesh):
    n_sec, n_dp = mesh.shape["section"], mesh.shape["dp"]
    token_blocks = P("section", "dp", None)
    rows = P("section", "dp")
    return jax.shard_map(
        functools.partial(local, n_sec, n_dp),
        mesh=mesh,
        in_specs=(token_blocks,) * 4 + (rows,) * 3,
        out_specs=(token_blocks,) * 4 + (rows,),
        check_vma=False,
    )
```

```python
import functools

import jax
import jax.numpy as jnp
from jax import lax
from jax.experimental import pallas as pl
from jax.experimental.pallas import tpu as pltpu
from jax.sharding import PartitionSpec as P

MESH = pl.DeviceIdType.MESH
F32 = jnp.float32
BF16 = jnp.bfloat16
ORDER = {
    2: ((0, 0), (1, 0)),
    8: ((0, 0), (0, 1), (1, 3), (0, 3), (1, 1), (0, 2), (1, 0), (1, 2)),
}
NN = (((1,), (0,)), ((), ()))
NT = (((1,), (1,)), ((), ()))
TN = (((0,), (0,)), ((), ()))


AHEAD_NEAR, AHEAD_FAR = 5, 0


def dot(a, b, dims):
    return lax.dot_general(a, b, dims, preferred_element_type=F32)


def kernel(
    n_sec,
    n_dp,
    x_hbm,
    st_hbm,
    gr_hbm,
    w_ref,
    gain_ref,
    fdoc_ref,
    bdoc_ref,
    handed,
    returned,
    parked,
    pgrad,
    ggrad,
    xv,
    sv,
    xf,
    xb,
    gb,
    fwd_out,
    bwd_out,
    dxh,
    dab,
    nb,
    vb,
    pr,
    ab,
    dproj,
    dg,
    zero,
    pf_own,
    pb_own,
    pf,
    pb,
    sums,
    total,
    loc_sem,
    xf_s,
    xf_r,
    xb_s,
    xb_r,
    gb_s,
    gb_r,
    pf_s,
    pf_r,
    pb_s,
    pb_r,
    ho_s,
    ho_r,
    re_s,
    re_r,
    su_s,
    su_r,
    pa_s,
    pa_r,
):
    tokens, width = x_hbm.shape
    cols = width // n_dp
    hd = w_ref.shape[1] // 4
    heads = cols // hd
    scale = hd ** (-0.5)
    s = lax.axis_index("section")
    g = lax.axis_index("dp")
    mirror = n_sec - 1 - s
    nxt = lax.rem(s + 1, n_sec)
    prv = lax.rem(s + n_sec - 1, n_sec)

    z = lax.div(s, 4)
    near = (lax.rem(z, 4) == 0) | (lax.rem(z, 4) == 3)
    ahead = jnp.where(near, AHEAD_NEAR, AHEAD_FAR)

    def span(j):
        return pl.ds(pl.multiple_of(j * cols, 128), cols)

    def remote(src, dst, ss, rs, dev):
        return pltpu.make_async_remote_copy(
            src_ref=src,
            dst_ref=dst,
            send_sem=ss,
            recv_sem=rs,
            device_id=dev,
            device_id_type=MESH,
        )

    ring = n_dp // 2
    x_lo, y = lax.div(g, ring), lax.rem(g, ring)
    way = 1 - 2 * lax.rem(s, 2)

    def pick(k, table):
        value = jnp.int32(table[0])
        for i in range(1, len(table)):
            value = jnp.where(k == i, table[i], value)
        return value

    def peer(k, sign):
        flip = pick(k, [a for a, _ in ORDER[n_dp]])
        turn = pick(k, [b for _, b in ORDER[n_dp]])
        across = x_lo + flip - 2 * x_lo * flip
        return across * ring + lax.rem(y + sign * turn + ring, ring)

    def each(first, body):
        def step(k, _):
            body(peer(k, way))
            return 0

        lax.fori_loop(first, n_dp, step, 0)

    def xf_copy(j):
        return remote(x_hbm.at[:, span(j)], xf.at[g], xf_s.at[j], xf_r.at[g], (s, j))

    def gb_copy(j):
        return remote(gr_hbm.at[:, span(j)], gb.at[g], gb_s.at[j], gb_r.at[g], (s, j))

    def xb_copy(j):
        return remote(st_hbm.at[:, span(j)], xb.at[g], xb_s.at[j], xb_r.at[g], (mirror, j))

    def pf_copy(j):
        return remote(pf_own, pf.at[g], pf_s.at[j], pf_r.at[g], (s, j))

    def pb_copy(j):
        return remote(pb_own, pb.at[g], pb_s.at[j], pb_r.at[g], (mirror, j))

    def ho_copy(j):
        return remote(fwd_out.at[j], handed.at[:, span(g)], ho_s.at[j], ho_r.at[g], (nxt, j))

    def re_copy(j):
        return remote(bwd_out.at[j], returned.at[:, span(g)], re_s.at[j], re_r.at[g], (prv, j))

    def su_copy(j):
        return remote(sums.at[g], sums.at[g], su_s.at[j], su_r.at[g], (s, j))

    def pa_copy(j):
        return remote(x_hbm.at[:, span(j)], parked.at[:, span(j)], pa_s.at[j], pa_r.at[j], (mirror, g))

    def xf_in(j):
        return remote(x_hbm.at[:, span(j)], xf.at[j], xf_s.at[j], xf_r.at[j], (s, j))

    def gb_in(j):
        return remote(gr_hbm.at[:, span(j)], gb.at[j], gb_s.at[j], gb_r.at[j], (s, j))

    def xb_in(j):
        return remote(st_hbm.at[:, span(j)], xb.at[j], xb_s.at[j], xb_r.at[j], (mirror, j))

    def pf_in(j):
        return remote(pf_own, pf.at[j], pf_s.at[j], pf_r.at[j], (s, j))

    def pb_in(j):
        return remote(pb_own, pb.at[j], pb_s.at[j], pb_r.at[j], (mirror, j))

    def ho_in(j):
        return remote(fwd_out.at[j], handed.at[:, span(j)], ho_s.at[j], ho_r.at[j], (nxt, j))

    def re_in(j):
        return remote(bwd_out.at[j], returned.at[:, span(j)], re_s.at[j], re_r.at[j], (prv, j))

    def su_in(j):
        return remote(sums.at[j], sums.at[j], su_s.at[j], su_r.at[j], (s, j))

    x_load = pltpu.make_async_copy(x_hbm, xv, loc_sem.at[0])
    s_load = pltpu.make_async_copy(st_hbm, sv, loc_sem.at[1])
    xf_load = pltpu.make_async_copy(x_hbm.at[:, span(g)], xf.at[g], loc_sem.at[2])
    gb_load = pltpu.make_async_copy(gr_hbm.at[:, span(g)], gb.at[g], loc_sem.at[3])
    s_load.start()
    x_load.start()
    xf_load.start()
    gb_load.start()

    barrier = pltpu.get_barrier_semaphore()

    def greet(k, _):
        for section in (mirror, nxt, prv):
            pl.semaphore_signal(barrier, inc=1, device_id=(section, k), device_id_type=MESH)
        return 0

    lax.fori_loop(0, n_dp, greet, 0)
    each(
        1,
        lambda j: pl.semaphore_signal(barrier, inc=1, device_id=(s, j), device_id_type=MESH),
    )
    pl.semaphore_wait(barrier, 4 * n_dp - 1)

    each(1, lambda j: xf_copy(j).start())
    xb_copy(g).start()

    def both(j):
        xb_copy(j).start()
        gb_copy(j).start()

    each(1, both)

    lanes = lax.broadcasted_iota(jnp.int32, (tokens, 128), 1)
    rows8 = lax.broadcasted_iota(jnp.int32, (8, 128), 0)
    chunk = 512

    def statistics(ref):
        def lane_sum(fn):
            def step(c, acc):
                part = ref[:, pl.ds(pl.multiple_of(c * chunk, chunk), chunk)].astype(F32)
                part = fn(part)
                for i in range(chunk // 128):
                    acc = acc + part[:, i * 128 : (i + 1) * 128]
                return acc

            acc = lax.fori_loop(0, width // chunk, step, jnp.zeros((tokens, 128), F32))
            return jnp.sum(acc, axis=1, keepdims=True)

        mean = lane_sum(lambda v: v) / width

        def squared(v):
            return (v - mean) * (v - mean)

        rstd = lax.rsqrt(lane_sum(squared) / width + 1e-05)
        both = jnp.where(lanes == 0, mean, jnp.where(lanes == 1, rstd, 0.0))
        return both.T[0:8, :]

    s_load.wait()
    pb_own[...] = statistics(sv)
    each(0, lambda j: pb_copy(j).start())
    x_load.wait()
    own = statistics(xv)
    own = jnp.where(rows8 == 2, jnp.broadcast_to(fdoc_ref[...].astype(F32), (8, 128)), own)
    own = jnp.where(rows8 == 3, jnp.broadcast_to(bdoc_ref[...].astype(F32), (8, 128)), own)
    pf_own[...] = own
    pf[g] = own
    each(1, lambda j: pf_copy(j).start())

    row_ids = lax.broadcasted_iota(jnp.int32, (tokens, tokens), 0)
    col_ids = lax.broadcasted_iota(jnp.int32, (tokens, tokens), 1)
    causal = col_ids <= row_ids

    def wide(row):
        return jnp.broadcast_to(row, (128, 128)).T

    def allowed_of(docs):
        across = jnp.broadcast_to(docs, (128, 128))
        return causal & (across == across.T)

    ats = [slice(h * hd, (h + 1) * hd) for h in range(heads)]
    three = [slice(h * 3 * hd, (h + 1) * 3 * hd) for h in range(heads)]

    def projections(normed, at):
        projected = dot(normed, w_ref[at, : 3 * hd], NN)
        return (
            (projected[:, :hd] * scale).astype(BF16),
            projected[:, hd : 2 * hd].astype(BF16),
            projected[:, 2 * hd :].astype(BF16),
        )

    def probabilities(q, k, allowed):
        e = jnp.where(allowed, jnp.exp(dot(q, k, NT)), 0.0)
        return e * (1.0 / jnp.sum(e, axis=-1, keepdims=True))

    xf_load.wait()
    gb_load.wait()

    def forward(k, _):
        j = peer(k, -way)

        @pl.when(k > 0)
        def _():
            pf_in(j).wait_recv()
            xf_in(j).wait_recv()

        mean = wide(pf[j, 0:1, :])
        rstd = wide(pf[j, 1:2, :])
        allowed = allowed_of(pf[j, 2:3, :])
        qkv, probs, attended = [], [], []
        for at in ats:
            x = xf[j, :, at].astype(F32)
            normed = ((x - mean) * rstd * gain_ref[:, at].astype(F32)).astype(BF16)
            qkv.append(projections(normed, at))
        for q, key, v in qkv:
            probs.append(probabilities(q, key, allowed).astype(BF16))
        for p, (q, key, v) in zip(probs, qkv):
            attended.append(dot(p, v, NN).astype(BF16))
        for at, a in zip(ats, attended):
            x = xf[j, :, at].astype(F32)
            fwd_out[j, :, at] = (x + dot(a, w_ref[at, 3 * hd :], NT)).astype(BF16)
        ho_copy(j).start()
        return 0

    lax.fori_loop(0, n_dp, forward, 0)

    def park(k, _):
        j = peer(k, way)
        xb_copy(j).wait_send()

        @pl.when(k < ahead)
        def _():
            pa_copy(j).start()
        return 0

    lax.fori_loop(0, n_dp, park, 0)

    def early(k, _):
        j = peer(k, -way)

        @pl.when(k > 0)
        def _():
            gb_in(j).wait_recv()

        for at in ats:
            dab[j, :, at] = dot(gb[j, :, at], w_ref[at, 3 * hd :], NN).astype(BF16)
        return 0

    lax.fori_loop(0, n_dp, early, 0)
    dg[...] = jnp.zeros_like(dg)
    group_ids = lax.broadcasted_iota(jnp.int32, (n_dp, 128), 0)

    def backward(k, parts):
        j = peer(k, way)
        pb_in(j).wait_recv()
        xb_in(j).wait_recv()
        mean = wide(pb[j, 0:1, :])
        rstd = wide(pb[j, 1:2, :])
        allowed = allowed_of(pf[j, 3:4, :])
        qkv, probs, dscores = [], [], []
        for at in ats:
            gain = gain_ref[:, at].astype(F32)
            normed = ((xb[j, :, at].astype(F32) - mean) * rstd * gain).astype(BF16)
            nb[j, :, at] = normed
            qkv.append(projections(normed, at))
            vb[j, :, at] = qkv[-1][2]
        for at, (q, key, v) in zip(ats, qkv):
            probs.append(probabilities(q, key, allowed))
            pr[j, :, at] = probs[-1].astype(BF16)
        for h, at in enumerate(ats):
            p, p16, da = probs[h], probs[h].astype(BF16), dab[j, :, at]
            dp = dot(da, qkv[h][2], NT)
            dscores.append((p * (dp - jnp.sum(dp * p, axis=-1, keepdims=True))).astype(BF16))
            start = three[h].start
            dproj[j, :, start + 2 * hd : start + 3 * hd] = dot(p16, da, TN).astype(BF16)
        for h in range(heads):
            q, key, v = qkv[h]
            start = three[h].start
            dproj[j, :, start : start + hd] = (dot(dscores[h], key, NN) * scale).astype(BF16)
            dproj[j, :, start + hd : start + 2 * hd] = dot(dscores[h], q, TN).astype(BF16)
        first = jnp.zeros((tokens, hd), F32)
        second = jnp.zeros((tokens, hd), F32)
        for h, at in enumerate(ats):
            xhat = (xb[j, :, at].astype(F32) - mean) * rstd
            dn = dot(dproj[j, :, three[h]], w_ref[at, : 3 * hd], NT)
            dg[0:1, at] += jnp.sum(dn * xhat, axis=0, keepdims=True)
            back = dn * gain_ref[:, at].astype(F32)
            dxh[j, :, at] = back
            first = first + back
            second = second + back * xhat
        here = group_ids == j
        return (
            jnp.where(here, jnp.sum(first.T, axis=0, keepdims=True), parts[0]),
            jnp.where(here, jnp.sum(second.T, axis=0, keepdims=True), parts[1]),
        )

    blank = jnp.zeros((n_dp, 128), F32)
    parts = lax.fori_loop(0, n_dp, backward, (blank, blank))
    sums[g, 0] = parts[0]
    sums[g, 1] = parts[1]

    each(1, lambda j: su_copy(j).start())
    each(1, lambda j: su_in(j).wait_recv())
    acc = sums[0]
    for i in range(1, n_dp):
        acc = acc + sums[i]
    total[...] = acc * (1.0 / width)

    @pl.when(s > 0)
    def _():
        def finish(k, _):
            j = peer(k, way)
            mean = wide(pb[j, 0:1, :])
            rstd = wide(pb[j, 1:2, :])
            here = group_ids == j
            c1 = wide(jnp.sum(jnp.where(here, total[0], 0.0), axis=0, keepdims=True))
            c2 = wide(jnp.sum(jnp.where(here, total[1], 0.0), axis=0, keepdims=True))
            for h in range(heads):
                at = slice(h * hd, (h + 1) * hd)
                xhat = (xb[j, :, at].astype(F32) - mean) * rstd
                back = rstd * (dxh[j, :, at] - c1 - xhat * c2)
                bwd_out[j, :, at] = (gb[j, :, at].astype(F32) + back).astype(BF16)
            re_copy(j).start()

            @pl.when(k >= ahead)
            def _():
                pa_copy(j).start()

            return 0

        lax.fori_loop(0, n_dp, finish, 0)

    @pl.when(s == 0)
    def _():
        def rest(k, _):
            pa_copy(peer(k, way)).start()
            return 0

        lax.fori_loop(ahead, n_dp, rest, 0)

    @pl.when(s == n_sec - 1)
    def _():
        zero[...] = jnp.zeros_like(zero)

        def fill(j):
            return pltpu.make_async_copy(zero, returned.at[:, span(j)], re_r.at[j])

        each(0, lambda j: fill(j).start())
        each(0, lambda j: fill(j).wait())

    def attend(j, _):
        for at in ats:
            ab[j, :, at] = dot(pr[j, :, at], vb[j, :, at], NN).astype(BF16)
        return 0

    lax.fori_loop(0, n_dp, attend, 0)
    every = n_dp * tokens
    for h, at in enumerate(ats):
        normed = nb[:, :, at].reshape(every, hd)
        into = dot(normed, dproj[:, :, three[h]].reshape(every, 3 * hd), TN)
        pgrad[at, : 3 * hd] = (into * (1.0 / n_dp)).astype(BF16)
        dy = gb[:, :, at].reshape(every, hd)
        out = dot(dy, ab[:, :, at].reshape(every, hd), TN)
        pgrad[at, 3 * hd :] = (out * (1.0 / n_dp)).astype(BF16)
    ggrad[...] = (dg[0:1, :] * (1.0 / n_dp)).astype(BF16)

    each(0, lambda j: ho_in(j).wait_recv())

    @pl.when(s < n_sec - 1)
    def _():
        each(0, lambda j: re_in(j).wait_recv())

    each(0, lambda j: pa_copy(j).wait_recv())
    each(1, lambda j: xf_copy(j).wait_send())
    each(1, lambda j: gb_copy(j).wait_send())
    each(1, lambda j: pf_copy(j).wait_send())
    each(0, lambda j: pb_copy(j).wait_send())
    each(1, lambda j: su_copy(j).wait_send())
    each(0, lambda j: ho_copy(j).wait_send())

    @pl.when(s > 0)
    def _():
        each(0, lambda j: re_copy(j).wait_send())

    each(0, lambda j: pa_copy(j).wait_send())


def local(n_sec, n_dp, inputs, stash, grad_in, proj, gain, fwd_docs, bwd_docs):
    tokens, width = inputs.shape[1:]
    rows, four = proj.shape[1:]
    blocks = (n_dp, tokens, rows)
    row_sem = pltpu.SemaphoreType.DMA((n_dp,))
    anywhere = pl.BlockSpec(memory_space=pl.ANY)
    vmem = pl.BlockSpec(memory_space=pltpu.VMEM)
    handed, returned, parked, pgrad, ggrad = pl.pallas_call(
        functools.partial(kernel, n_sec, n_dp),
        out_shape=[jax.ShapeDtypeStruct((tokens, width), BF16)] * 3
        + [
            jax.ShapeDtypeStruct((rows, four), BF16),
            jax.ShapeDtypeStruct((1, rows), BF16),
        ],
        in_specs=[anywhere] * 3 + [vmem] * 4,
        out_specs=[anywhere] * 3 + [vmem] * 2,
        scratch_shapes=[
            pltpu.VMEM((tokens, width), BF16),
            pltpu.VMEM((tokens, width), BF16),
            pltpu.VMEM(blocks, BF16),
            pltpu.VMEM(blocks, BF16),
            pltpu.VMEM(blocks, BF16),
            pltpu.VMEM(blocks, BF16),
            pltpu.VMEM(blocks, BF16),
            pltpu.VMEM(blocks, F32),
            pltpu.VMEM(blocks, BF16),
            pltpu.VMEM(blocks, BF16),
            pltpu.VMEM(blocks, BF16),
            pltpu.VMEM(blocks, BF16),
            pltpu.VMEM(blocks, BF16),
            pltpu.VMEM((n_dp, tokens, 3 * rows), BF16),
            pltpu.VMEM((8, rows), F32),
            pltpu.VMEM((tokens, rows), BF16),
            pltpu.VMEM((8, 128), F32),
            pltpu.VMEM((8, 128), F32),
            pltpu.VMEM((n_dp, 8, 128), F32),
            pltpu.VMEM((n_dp, 8, 128), F32),
            pltpu.VMEM((n_dp, 2, n_dp, 128), F32),
            pltpu.VMEM((2, n_dp, 128), F32),
            pltpu.SemaphoreType.DMA((4,)),
        ]
        + [row_sem] * 18,
        compiler_params=pltpu.CompilerParams(
            collective_id=0, has_side_effects=True, vmem_limit_bytes=48 * 1024 * 1024
        ),
    )(inputs[0], stash[0], grad_in[0], proj[0], gain, fwd_docs, bwd_docs)
    return handed[None], returned[None], parked[None], pgrad[None], ggrad


def solution(mesh):
    n_sec, n_dp = mesh.shape["section"], mesh.shape["dp"]
    token_blocks = P("section", "dp", None)
    rows = P("section", "dp")
    return jax.shard_map(
        functools.partial(local, n_sec, n_dp),
        mesh=mesh,
        in_specs=(token_blocks,) * 4 + (rows,) * 3,
        out_specs=(token_blocks,) * 4 + (rows,),
        check_vma=False,
    )
```

```python
import functools

import jax
import jax.numpy as jnp
from jax import lax
from jax.experimental import pallas as pl
from jax.experimental.pallas import tpu as pltpu
from jax.sharding import PartitionSpec as P

MESH = pl.DeviceIdType.MESH
F32 = jnp.float32
BF16 = jnp.bfloat16
ORDER = {
    2: ((0, 0), (1, 0)),
    8: ((0, 0), (0, 1), (1, 3), (0, 3), (1, 1), (0, 2), (1, 0), (1, 2)),
}
FIRST = {2: 0, 8: 6}
NN = (((1,), (0,)), ((), ()))
NT = (((1,), (1,)), ((), ()))
TN = (((0,), (0,)), ((), ()))


def dot(a, b, dims):
    return lax.dot_general(a, b, dims, preferred_element_type=F32)


def kernel(
    n_sec,
    n_dp,
    x_hbm,
    st_hbm,
    gr_hbm,
    w_ref,
    gain_ref,
    fdoc_ref,
    bdoc_ref,
    handed,
    returned,
    parked,
    pgrad,
    ggrad,
    xv,
    sv,
    xf,
    xb,
    gb,
    fwd_out,
    bwd_out,
    dxh,
    dab,
    nb,
    vb,
    pr,
    ab,
    dproj,
    dg,
    zero,
    pf_own,
    pb_own,
    pf,
    pb,
    sums,
    total,
    loc_sem,
    xf_s,
    xf_r,
    xb_s,
    xb_r,
    gb_s,
    gb_r,
    pf_s,
    pf_r,
    pb_s,
    pb_r,
    ho_s,
    ho_r,
    re_s,
    re_r,
    su_s,
    su_r,
    pa_s,
    pa_r,
    vi_s,
    vi_r,
    via,
):
    tokens, width = x_hbm.shape
    cols = width // n_dp
    hd = w_ref.shape[1] // 4
    heads = cols // hd
    scale = hd ** (-0.5)
    s = lax.axis_index("section")
    g = lax.axis_index("dp")
    mirror = n_sec - 1 - s
    nxt = lax.rem(s + 1, n_sec)
    prv = lax.rem(s + n_sec - 1, n_sec)

    z = lax.div(s, 4)
    near = (lax.rem(z, 4) == 0) | (lax.rem(z, 4) == 3)
    half = n_sec // 2
    h_from = lax.rem(s, half) == half - 1
    h_via = lax.rem(s, half) == half - 3
    h_to = lax.rem(s, half) == 0
    r_from, r_via, r_to = s == half, s == half + 2, s == half - 1

    ahead = jnp.where(near & (lax.rem(s, 4) != 0), n_dp, 0)
    ahead = jnp.where(lax.rem(s, half) == 4, 3, ahead)

    def detour(j):
        return lax.rem(g + n_dp - j, ring) == 0

    def span(j):
        return pl.ds(pl.multiple_of(j * cols, 128), cols)

    def remote(src, dst, ss, rs, dev):
        return pltpu.make_async_remote_copy(
            src_ref=src,
            dst_ref=dst,
            send_sem=ss,
            recv_sem=rs,
            device_id=dev,
            device_id_type=MESH,
        )

    ring = n_dp // 2
    x_lo, y = lax.div(g, ring), lax.rem(g, ring)
    way = 1 - 2 * lax.rem(s, 2)

    def pick(k, table):
        value = jnp.int32(table[0])
        for i in range(1, len(table)):
            value = jnp.where(k == i, table[i], value)
        return value

    def peer(k, sign):
        flip = pick(k, [a for a, _ in ORDER[n_dp]])
        turn = pick(k, [b for _, b in ORDER[n_dp]])
        across = x_lo + flip - 2 * x_lo * flip
        return across * ring + lax.rem(y + sign * turn + ring, ring)

    def each(first, body):
        def step(k, _):
            body(peer(k, way))
            return 0

        lax.fori_loop(first, n_dp, step, 0)

    def xf_copy(j):
        return remote(x_hbm.at[:, span(j)], xf.at[g], xf_s.at[j], xf_r.at[g], (s, j))

    def gb_copy(j):
        return remote(gr_hbm.at[:, span(j)], gb.at[g], gb_s.at[j], gb_r.at[g], (s, j))

    def xb_copy(j):
        return remote(st_hbm.at[:, span(j)], xb.at[g], xb_s.at[j], xb_r.at[g], (mirror, j))

    def pf_copy(j):
        return remote(pf_own, pf.at[g], pf_s.at[j], pf_r.at[g], (s, j))

    def pb_copy(j):
        return remote(pb_own, pb.at[g], pb_s.at[j], pb_r.at[g], (mirror, j))

    def ho_copy(j):
        return remote(fwd_out.at[j], handed.at[:, span(g)], ho_s.at[j], ho_r.at[g], (nxt, j))

    def re_copy(j):
        return remote(bwd_out.at[j], returned.at[:, span(g)], re_s.at[j], re_r.at[g], (prv, j))

    def ho_first(j):
        return remote(fwd_out.at[j], via.at[g], ho_s.at[j], vi_r.at[g], (s - 2, j))

    def ho_second(j):
        return remote(via.at[j], handed.at[:, span(j)], vi_s.at[j], ho_r.at[j], (lax.rem(s + 3, n_sec), g))

    def re_first(j):
        return remote(bwd_out.at[j], via.at[g], re_s.at[j], vi_r.at[g], (s + 2, j))

    def re_second(j):
        return remote(via.at[j], returned.at[:, span(j)], vi_s.at[j], re_r.at[j], (s - 3, g))

    def vi_in(j):
        return remote(fwd_out.at[j], via.at[j], ho_s.at[j], vi_r.at[j], (s, j))

    def forward_by(second):
        def step(j):
            @pl.when(detour(j))
            def _():
                vi_in(j).wait_recv()
                second(j).start()

        each(0, step)

    def forwarded(second):
        def step(j):
            @pl.when(detour(j))
            def _():
                second(j).wait_send()

        each(0, step)

    def su_copy(j):
        return remote(sums.at[g], sums.at[g], su_s.at[j], su_r.at[g], (s, j))

    def pa_copy(j):
        return remote(x_hbm.at[:, span(j)], parked.at[:, span(j)], pa_s.at[j], pa_r.at[j], (mirror, g))

    def xf_in(j):
        return remote(x_hbm.at[:, span(j)], xf.at[j], xf_s.at[j], xf_r.at[j], (s, j))

    def gb_in(j):
        return remote(gr_hbm.at[:, span(j)], gb.at[j], gb_s.at[j], gb_r.at[j], (s, j))

    def xb_in(j):
        return remote(st_hbm.at[:, span(j)], xb.at[j], xb_s.at[j], xb_r.at[j], (mirror, j))

    def pf_in(j):
        return remote(pf_own, pf.at[j], pf_s.at[j], pf_r.at[j], (s, j))

    def pb_in(j):
        return remote(pb_own, pb.at[j], pb_s.at[j], pb_r.at[j], (mirror, j))

    def ho_in(j):
        return remote(fwd_out.at[j], handed.at[:, span(j)], ho_s.at[j], ho_r.at[j], (nxt, j))

    def re_in(j):
        return remote(bwd_out.at[j], returned.at[:, span(j)], re_s.at[j], re_r.at[j], (prv, j))

    def su_in(j):
        return remote(sums.at[j], sums.at[j], su_s.at[j], su_r.at[j], (s, j))

    x_load = pltpu.make_async_copy(x_hbm, xv, loc_sem.at[0])
    s_load = pltpu.make_async_copy(st_hbm, sv, loc_sem.at[1])
    xf_load = pltpu.make_async_copy(x_hbm.at[:, span(g)], xf.at[g], loc_sem.at[2])
    gb_load = pltpu.make_async_copy(gr_hbm.at[:, span(g)], gb.at[g], loc_sem.at[3])
    s_load.start()
    x_load.start()
    xf_load.start()
    gb_load.start()

    barrier = pltpu.get_barrier_semaphore()

    def greet(k, _):
        for section in (mirror, nxt, prv):
            pl.semaphore_signal(barrier, inc=1, device_id=(section, k), device_id_type=MESH)
        return 0

    lax.fori_loop(0, n_dp, greet, 0)
    each(
        1,
        lambda j: pl.semaphore_signal(barrier, inc=1, device_id=(s, j), device_id_type=MESH),
    )

    def greet_row(section):
        def one(k, _):
            pl.semaphore_signal(barrier, inc=1, device_id=(section, k), device_id_type=MESH)
            return 0

        lax.fori_loop(0, n_dp, one, 0)

    def greet_one(section):
        pl.semaphore_signal(barrier, inc=1, device_id=(section, g), device_id_type=MESH)

    pl.when(h_from)(lambda: greet_row(s - 2))
    pl.when(h_via)(lambda: greet_row(s + 2))
    pl.when(h_via)(lambda: greet_one(lax.rem(s + 3, n_sec)))
    pl.when(h_to)(lambda: greet_one(lax.rem(s + n_sec - 3, n_sec)))
    pl.when(r_from)(lambda: greet_row(s + 2))
    pl.when(r_via)(lambda: greet_row(s - 2))
    pl.when(r_via)(lambda: greet_one(s - 3))
    pl.when(r_to)(lambda: greet_one(s + 3))

    def count(*roles):
        return sum(role.astype(jnp.int32) for role in roles)

    rows_met = count(h_from, h_via, r_from, r_via)
    ones_met = count(h_via, h_to, r_via, r_to)
    pl.semaphore_wait(barrier, 4 * n_dp - 1 + n_dp * rows_met + ones_met)

    each(1, lambda j: xf_copy(j).start())
    xb_copy(g).start()

    def both(j):
        xb_copy(j).start()
        gb_copy(j).start()

    each(1, both)

    lanes = lax.broadcasted_iota(jnp.int32, (tokens, 128), 1)
    rows8 = lax.broadcasted_iota(jnp.int32, (8, 128), 0)
    chunk = 512

    def statistics(ref):
        def lane_sum(fn):
            def step(c, acc):
                part = ref[:, pl.ds(pl.multiple_of(c * chunk, chunk), chunk)].astype(F32)
                part = fn(part)
                for i in range(chunk // 128):
                    acc = acc + part[:, i * 128 : (i + 1) * 128]
                return acc

            acc = lax.fori_loop(0, width // chunk, step, jnp.zeros((tokens, 128), F32))
            return jnp.sum(acc, axis=1, keepdims=True)

        mean = lane_sum(lambda v: v) / width

        def squared(v):
            return (v - mean) * (v - mean)

        rstd = lax.rsqrt(lane_sum(squared) / width + 1e-05)
        both = jnp.where(lanes == 0, mean, jnp.where(lanes == 1, rstd, 0.0))
        return both.T[0:8, :]

    s_load.wait()
    pb_own[...] = statistics(sv)
    each(0, lambda j: pb_copy(j).start())
    x_load.wait()
    own = statistics(xv)
    own = jnp.where(rows8 == 2, jnp.broadcast_to(fdoc_ref[...].astype(F32), (8, 128)), own)
    own = jnp.where(rows8 == 3, jnp.broadcast_to(bdoc_ref[...].astype(F32), (8, 128)), own)
    pf_own[...] = own
    pf[g] = own
    each(1, lambda j: pf_copy(j).start())

    row_ids = lax.broadcasted_iota(jnp.int32, (tokens, tokens), 0)
    col_ids = lax.broadcasted_iota(jnp.int32, (tokens, tokens), 1)
    causal = col_ids <= row_ids

    def wide(row):
        return jnp.broadcast_to(row, (128, 128)).T

    def allowed_of(docs):
        across = jnp.broadcast_to(docs, (128, 128))
        return causal & (across == across.T)

    ats = [slice(h * hd, (h + 1) * hd) for h in range(heads)]
    three = [slice(h * 3 * hd, (h + 1) * 3 * hd) for h in range(heads)]

    def projections(normed, at):
        projected = dot(normed, w_ref[at, : 3 * hd], NN)
        return (
            (projected[:, :hd] * scale).astype(BF16),
            projected[:, hd : 2 * hd].astype(BF16),
            projected[:, 2 * hd :].astype(BF16),
        )

    def probabilities(q, k, allowed):
        e = jnp.where(allowed, jnp.exp(dot(q, k, NT)), 0.0)
        return e * (1.0 / jnp.sum(e, axis=-1, keepdims=True))

    xf_load.wait()
    gb_load.wait()

    def forward(k, _):
        j = peer(k, -way)

        @pl.when(k > 0)
        def _():
            pf_in(j).wait_recv()
            xf_in(j).wait_recv()

        mean = wide(pf[j, 0:1, :])
        rstd = wide(pf[j, 1:2, :])
        allowed = allowed_of(pf[j, 2:3, :])
        qkv, probs, attended = [], [], []
        for at in ats:
            x = xf[j, :, at].astype(F32)
            normed = ((x - mean) * rstd * gain_ref[:, at].astype(F32)).astype(BF16)
            qkv.append(projections(normed, at))
        for q, key, v in qkv:
            probs.append(probabilities(q, key, allowed).astype(BF16))
        for p, (q, key, v) in zip(probs, qkv):
            attended.append(dot(p, v, NN).astype(BF16))
        for at, a in zip(ats, attended):
            x = xf[j, :, at].astype(F32)
            fwd_out[j, :, at] = (x + dot(a, w_ref[at, 3 * hd :], NT)).astype(BF16)
        aside = h_from & detour(j)

        @pl.when(aside)
        def _():
            ho_first(j).start()

        @pl.when(jnp.logical_not(aside))
        def _():
            ho_copy(j).start()

        return 0

    lax.fori_loop(0, n_dp, forward, 0)

    def park(k, _):
        j = peer(k, way)
        xb_copy(j).wait_send()

        @pl.when(k < ahead)
        def _():
            pa_copy(j).start()
        return 0

    lax.fori_loop(0, n_dp, park, 0)

    def early(k, _):
        j = peer(k, -way)

        @pl.when(k > 0)
        def _():
            gb_in(j).wait_recv()

        for at in ats:
            dab[j, :, at] = dot(gb[j, :, at], w_ref[at, 3 * hd :], NN).astype(BF16)
        return 0

    lax.fori_loop(0, n_dp, early, 0)
    dg[...] = jnp.zeros_like(dg)
    group_ids = lax.broadcasted_iota(jnp.int32, (n_dp, 128), 0)

    def backward(k, parts):
        j = peer(k, way)
        pb_in(j).wait_recv()
        xb_in(j).wait_recv()
        mean = wide(pb[j, 0:1, :])
        rstd = wide(pb[j, 1:2, :])
        allowed = allowed_of(pf[j, 3:4, :])
        qkv, probs, dscores = [], [], []
        for at in ats:
            gain = gain_ref[:, at].astype(F32)
            normed = ((xb[j, :, at].astype(F32) - mean) * rstd * gain).astype(BF16)
            nb[j, :, at] = normed
            qkv.append(projections(normed, at))
            vb[j, :, at] = qkv[-1][2]
        for at, (q, key, v) in zip(ats, qkv):
            probs.append(probabilities(q, key, allowed))
            pr[j, :, at] = probs[-1].astype(BF16)
        for h, at in enumerate(ats):
            p, p16, da = probs[h], probs[h].astype(BF16), dab[j, :, at]
            dp = dot(da, qkv[h][2], NT)
            dscores.append((p * (dp - jnp.sum(dp * p, axis=-1, keepdims=True))).astype(BF16))
            start = three[h].start
            dproj[j, :, start + 2 * hd : start + 3 * hd] = dot(p16, da, TN).astype(BF16)
        for h in range(heads):
            q, key, v = qkv[h]
            start = three[h].start
            dproj[j, :, start : start + hd] = (dot(dscores[h], key, NN) * scale).astype(BF16)
            dproj[j, :, start + hd : start + 2 * hd] = dot(dscores[h], q, TN).astype(BF16)
        first = jnp.zeros((tokens, hd), F32)
        second = jnp.zeros((tokens, hd), F32)
        for h, at in enumerate(ats):
            xhat = (xb[j, :, at].astype(F32) - mean) * rstd
            dn = dot(dproj[j, :, three[h]], w_ref[at, : 3 * hd], NT)
            dg[0:1, at] += jnp.sum(dn * xhat, axis=0, keepdims=True)
            back = dn * gain_ref[:, at].astype(F32)
            dxh[j, :, at] = back
            first = first + back
            second = second + back * xhat
        here = group_ids == j
        return (
            jnp.where(here, jnp.sum(first.T, axis=0, keepdims=True), parts[0]),
            jnp.where(here, jnp.sum(second.T, axis=0, keepdims=True), parts[1]),
        )

    blank = jnp.zeros((n_dp, 128), F32)
    parts = lax.fori_loop(0, n_dp, backward, (blank, blank))
    sums[g, 0] = parts[0]
    sums[g, 1] = parts[1]

    each(1, lambda j: su_copy(j).start())

    @pl.when(h_via)
    def _():
        forward_by(ho_second)

    each(1, lambda j: su_in(j).wait_recv())
    acc = sums[0]
    for i in range(1, n_dp):
        acc = acc + sums[i]
    total[...] = acc * (1.0 / width)

    @pl.when(s > 0)
    def _():
        def finish(k, _):
            j = peer(lax.rem(k + FIRST[n_dp], n_dp), way)
            mean = wide(pb[j, 0:1, :])
            rstd = wide(pb[j, 1:2, :])
            here = group_ids == j
            c1 = wide(jnp.sum(jnp.where(here, total[0], 0.0), axis=0, keepdims=True))
            c2 = wide(jnp.sum(jnp.where(here, total[1], 0.0), axis=0, keepdims=True))
            for h in range(heads):
                at = slice(h * hd, (h + 1) * hd)
                xhat = (xb[j, :, at].astype(F32) - mean) * rstd
                back = rstd * (dxh[j, :, at] - c1 - xhat * c2)
                bwd_out[j, :, at] = (gb[j, :, at].astype(F32) + back).astype(BF16)
            aside = r_from & detour(j)

            @pl.when(aside)
            def _():
                re_first(j).start()

            @pl.when(jnp.logical_not(aside))
            def _():
                re_copy(j).start()

            return 0

        lax.fori_loop(0, n_dp, finish, 0)

    @pl.when(r_via)
    def _():
        forward_by(re_second)

    def rest(k, _):
        pa_copy(peer(k, way)).start()
        return 0

    lax.fori_loop(ahead, n_dp, rest, 0)

    @pl.when(s == n_sec - 1)
    def _():
        zero[...] = jnp.zeros_like(zero)

        def fill(j):
            return pltpu.make_async_copy(zero, returned.at[:, span(j)], re_r.at[j])

        each(0, lambda j: fill(j).start())
        each(0, lambda j: fill(j).wait())

    def attend(j, _):
        for at in ats:
            ab[j, :, at] = dot(pr[j, :, at], vb[j, :, at], NN).astype(BF16)
        return 0

    lax.fori_loop(0, n_dp, attend, 0)
    every = n_dp * tokens
    for h, at in enumerate(ats):
        normed = nb[:, :, at].reshape(every, hd)
        into = dot(normed, dproj[:, :, three[h]].reshape(every, 3 * hd), TN)
        pgrad[at, : 3 * hd] = (into * (1.0 / n_dp)).astype(BF16)
        dy = gb[:, :, at].reshape(every, hd)
        out = dot(dy, ab[:, :, at].reshape(every, hd), TN)
        pgrad[at, 3 * hd :] = (out * (1.0 / n_dp)).astype(BF16)
    ggrad[...] = (dg[0:1, :] * (1.0 / n_dp)).astype(BF16)

    each(0, lambda j: ho_in(j).wait_recv())

    @pl.when(s < n_sec - 1)
    def _():
        each(0, lambda j: re_in(j).wait_recv())

    each(0, lambda j: pa_copy(j).wait_recv())
    @pl.when(h_via)
    def _():
        forwarded(ho_second)

    @pl.when(r_via)
    def _():
        forwarded(re_second)

    each(1, lambda j: xf_copy(j).wait_send())
    each(1, lambda j: gb_copy(j).wait_send())
    each(1, lambda j: pf_copy(j).wait_send())
    each(0, lambda j: pb_copy(j).wait_send())
    each(1, lambda j: su_copy(j).wait_send())
    each(0, lambda j: ho_copy(j).wait_send())

    @pl.when(s > 0)
    def _():
        each(0, lambda j: re_copy(j).wait_send())

    each(0, lambda j: pa_copy(j).wait_send())


def local(n_sec, n_dp, inputs, stash, grad_in, proj, gain, fwd_docs, bwd_docs):
    tokens, width = inputs.shape[1:]
    rows, four = proj.shape[1:]
    blocks = (n_dp, tokens, rows)
    row_sem = pltpu.SemaphoreType.DMA((n_dp,))
    anywhere = pl.BlockSpec(memory_space=pl.ANY)
    vmem = pl.BlockSpec(memory_space=pltpu.VMEM)
    handed, returned, parked, pgrad, ggrad = pl.pallas_call(
        functools.partial(kernel, n_sec, n_dp),
        out_shape=[jax.ShapeDtypeStruct((tokens, width), BF16)] * 3
        + [
            jax.ShapeDtypeStruct((rows, four), BF16),
            jax.ShapeDtypeStruct((1, rows), BF16),
        ],
        in_specs=[anywhere] * 3 + [vmem] * 4,
        out_specs=[anywhere] * 3 + [vmem] * 2,
        scratch_shapes=[
            pltpu.VMEM((tokens, width), BF16),
            pltpu.VMEM((tokens, width), BF16),
            pltpu.VMEM(blocks, BF16),
            pltpu.VMEM(blocks, BF16),
            pltpu.VMEM(blocks, BF16),
            pltpu.VMEM(blocks, BF16),
            pltpu.VMEM(blocks, BF16),
            pltpu.VMEM(blocks, F32),
            pltpu.VMEM(blocks, BF16),
            pltpu.VMEM(blocks, BF16),
            pltpu.VMEM(blocks, BF16),
            pltpu.VMEM(blocks, BF16),
            pltpu.VMEM(blocks, BF16),
            pltpu.VMEM((n_dp, tokens, 3 * rows), BF16),
            pltpu.VMEM((8, rows), F32),
            pltpu.VMEM((tokens, rows), BF16),
            pltpu.VMEM((8, 128), F32),
            pltpu.VMEM((8, 128), F32),
            pltpu.VMEM((n_dp, 8, 128), F32),
            pltpu.VMEM((n_dp, 8, 128), F32),
            pltpu.VMEM((n_dp, 2, n_dp, 128), F32),
            pltpu.VMEM((2, n_dp, 128), F32),
            pltpu.SemaphoreType.DMA((4,)),
        ]
        + [row_sem] * 20
        + [pltpu.VMEM(blocks, BF16)],
        compiler_params=pltpu.CompilerParams(
            collective_id=0, has_side_effects=True, vmem_limit_bytes=48 * 1024 * 1024
        ),
    )(inputs[0], stash[0], grad_in[0], proj[0], gain, fwd_docs, bwd_docs)
    return handed[None], returned[None], parked[None], pgrad[None], ggrad


def solution(mesh):
    n_sec, n_dp = mesh.shape["section"], mesh.shape["dp"]
    token_blocks = P("section", "dp", None)
    rows = P("section", "dp")
    return jax.shard_map(
        functools.partial(local, n_sec, n_dp),
        mesh=mesh,
        in_specs=(token_blocks,) * 4 + (rows,) * 3,
        out_specs=(token_blocks,) * 4 + (rows,),
        check_vma=False,
    )
```

```python
import functools

import jax
import jax.numpy as jnp
from jax import lax
from jax.experimental import pallas as pl
from jax.experimental.pallas import tpu as pltpu
from jax.sharding import PartitionSpec as P

MESH = pl.DeviceIdType.MESH
F32 = jnp.float32
BF16 = jnp.bfloat16
ORDER = {
    2: ((0, 0), (1, 0)),
    8: ((0, 0), (0, 1), (1, 3), (0, 3), (1, 1), (0, 2), (1, 0), (1, 2)),
}
FIRST = {2: 0, 8: 6}
NN = (((1,), (0,)), ((), ()))
NT = (((1,), (1,)), ((), ()))
TN = (((0,), (0,)), ((), ()))


def dot(a, b, dims):
    return lax.dot_general(a, b, dims, preferred_element_type=F32)


def kernel(
    n_sec,
    n_dp,
    x_hbm,
    st_hbm,
    gr_hbm,
    w_ref,
    gain_ref,
    fdoc_ref,
    bdoc_ref,
    handed,
    returned,
    parked,
    pgrad,
    ggrad,
    xv,
    sv,
    xf,
    xb,
    gb,
    fwd_out,
    bwd_out,
    dxh,
    dab,
    nb,
    vb,
    pr,
    ab,
    dproj,
    dg,
    zero,
    pf_own,
    pb_own,
    pf,
    pb,
    sums,
    total,
    loc_sem,
    xf_s,
    xf_r,
    xb_s,
    xb_r,
    gb_s,
    gb_r,
    pf_s,
    pf_r,
    pb_s,
    pb_r,
    ho_s,
    ho_r,
    re_s,
    re_r,
    su_s,
    su_r,
    pa_s,
    pa_r,
    vi_s,
    vi_r,
    via,
):
    tokens, width = x_hbm.shape
    cols = width // n_dp
    hd = w_ref.shape[1] // 4
    heads = cols // hd
    scale = hd ** (-0.5)
    s = lax.axis_index("section")
    g = lax.axis_index("dp")
    mirror = n_sec - 1 - s
    nxt = lax.rem(s + 1, n_sec)
    prv = lax.rem(s + n_sec - 1, n_sec)

    z = lax.div(s, 4)
    near = (lax.rem(z, 4) == 0) | (lax.rem(z, 4) == 3)
    half = n_sec // 2
    h_from = lax.rem(s, half) == half - 1
    h_via = lax.rem(s, half) == half - 3
    h_to = lax.rem(s, half) == 0
    r_from, r_via, r_to = s == half, s == half + 2, s == half - 1

    ahead = jnp.where(near & ((lax.rem(s, 4) != 0) | (s == 0)), n_dp, 0)
    ahead = jnp.where(lax.rem(s, half) == 4, 3, ahead)

    def detour(j):
        return lax.rem(g + n_dp - j, ring) == 0

    def span(j):
        return pl.ds(pl.multiple_of(j * cols, 128), cols)

    def remote(src, dst, ss, rs, dev):
        return pltpu.make_async_remote_copy(
            src_ref=src,
            dst_ref=dst,
            send_sem=ss,
            recv_sem=rs,
            device_id=dev,
            device_id_type=MESH,
        )

    ring = n_dp // 2
    x_lo, y = lax.div(g, ring), lax.rem(g, ring)
    way = 1 - 2 * lax.rem(s, 2)

    def pick(k, table):
        value = jnp.int32(table[0])
        for i in range(1, len(table)):
            value = jnp.where(k == i, table[i], value)
        return value

    def peer(k, sign):
        flip = pick(k, [a for a, _ in ORDER[n_dp]])
        turn = pick(k, [b for _, b in ORDER[n_dp]])
        across = x_lo + flip - 2 * x_lo * flip
        return across * ring + lax.rem(y + sign * turn + ring, ring)

    def each(first, body):
        def step(k, _):
            body(peer(k, way))
            return 0

        lax.fori_loop(first, n_dp, step, 0)

    def xf_copy(j):
        return remote(x_hbm.at[:, span(j)], xf.at[g], xf_s.at[j], xf_r.at[g], (s, j))

    def gb_copy(j):
        return remote(gr_hbm.at[:, span(j)], gb.at[g], gb_s.at[j], gb_r.at[g], (s, j))

    def xb_copy(j):
        return remote(st_hbm.at[:, span(j)], xb.at[g], xb_s.at[j], xb_r.at[g], (mirror, j))

    def pf_copy(j):
        return remote(pf_own, pf.at[g], pf_s.at[j], pf_r.at[g], (s, j))

    def pb_copy(j):
        return remote(pb_own, pb.at[g], pb_s.at[j], pb_r.at[g], (mirror, j))

    def ho_copy(j):
        return remote(fwd_out.at[j], handed.at[:, span(g)], ho_s.at[j], ho_r.at[g], (nxt, j))

    def re_copy(j):
        return remote(bwd_out.at[j], returned.at[:, span(g)], re_s.at[j], re_r.at[g], (prv, j))

    def ho_first(j):
        return remote(fwd_out.at[j], via.at[g], ho_s.at[j], vi_r.at[g], (s - 2, j))

    def ho_second(j):
        return remote(via.at[j], handed.at[:, span(j)], vi_s.at[j], ho_r.at[j], (lax.rem(s + 3, n_sec), g))

    def re_first(j):
        return remote(bwd_out.at[j], via.at[g], re_s.at[j], vi_r.at[g], (s + 2, j))

    def re_second(j):
        return remote(via.at[j], returned.at[:, span(j)], vi_s.at[j], re_r.at[j], (s - 3, g))

    def vi_in(j):
        return remote(fwd_out.at[j], via.at[j], ho_s.at[j], vi_r.at[j], (s, j))

    def forward_by(second):
        def step(j):
            @pl.when(detour(j))
            def _():
                vi_in(j).wait_recv()
                second(j).start()

        each(0, step)

    def forwarded(second):
        def step(j):
            @pl.when(detour(j))
            def _():
                second(j).wait_send()

        each(0, step)

    def su_copy(j):
        return remote(sums.at[g], sums.at[g], su_s.at[j], su_r.at[g], (s, j))

    def pa_copy(j):
        return remote(x_hbm.at[:, span(j)], parked.at[:, span(j)], pa_s.at[j], pa_r.at[j], (mirror, g))

    def xf_in(j):
        return remote(x_hbm.at[:, span(j)], xf.at[j], xf_s.at[j], xf_r.at[j], (s, j))

    def gb_in(j):
        return remote(gr_hbm.at[:, span(j)], gb.at[j], gb_s.at[j], gb_r.at[j], (s, j))

    def xb_in(j):
        return remote(st_hbm.at[:, span(j)], xb.at[j], xb_s.at[j], xb_r.at[j], (mirror, j))

    def pf_in(j):
        return remote(pf_own, pf.at[j], pf_s.at[j], pf_r.at[j], (s, j))

    def pb_in(j):
        return remote(pb_own, pb.at[j], pb_s.at[j], pb_r.at[j], (mirror, j))

    def ho_in(j):
        return remote(fwd_out.at[j], handed.at[:, span(j)], ho_s.at[j], ho_r.at[j], (nxt, j))

    def re_in(j):
        return remote(bwd_out.at[j], returned.at[:, span(j)], re_s.at[j], re_r.at[j], (prv, j))

    def su_in(j):
        return remote(sums.at[j], sums.at[j], su_s.at[j], su_r.at[j], (s, j))

    x_load = pltpu.make_async_copy(x_hbm, xv, loc_sem.at[0])
    s_load = pltpu.make_async_copy(st_hbm, sv, loc_sem.at[1])
    xf_load = pltpu.make_async_copy(x_hbm.at[:, span(g)], xf.at[g], loc_sem.at[2])
    gb_load = pltpu.make_async_copy(gr_hbm.at[:, span(g)], gb.at[g], loc_sem.at[3])
    s_load.start()
    x_load.start()
    xf_load.start()
    gb_load.start()

    barrier = pltpu.get_barrier_semaphore()

    def greet(k, _):
        for section in (mirror, nxt, prv):
            pl.semaphore_signal(barrier, inc=1, device_id=(section, k), device_id_type=MESH)
        return 0

    lax.fori_loop(0, n_dp, greet, 0)
    each(
        1,
        lambda j: pl.semaphore_signal(barrier, inc=1, device_id=(s, j), device_id_type=MESH),
    )

    def greet_row(section):
        def one(k, _):
            pl.semaphore_signal(barrier, inc=1, device_id=(section, k), device_id_type=MESH)
            return 0

        lax.fori_loop(0, n_dp, one, 0)

    def greet_one(section):
        pl.semaphore_signal(barrier, inc=1, device_id=(section, g), device_id_type=MESH)

    pl.when(h_from)(lambda: greet_row(s - 2))
    pl.when(h_via)(lambda: greet_row(s + 2))
    pl.when(h_via)(lambda: greet_one(lax.rem(s + 3, n_sec)))
    pl.when(h_to)(lambda: greet_one(lax.rem(s + n_sec - 3, n_sec)))
    pl.when(r_from)(lambda: greet_row(s + 2))
    pl.when(r_via)(lambda: greet_row(s - 2))
    pl.when(r_via)(lambda: greet_one(s - 3))
    pl.when(r_to)(lambda: greet_one(s + 3))

    def count(*roles):
        return sum(role.astype(jnp.int32) for role in roles)

    rows_met = count(h_from, h_via, r_from, r_via)
    ones_met = count(h_via, h_to, r_via, r_to)
    pl.semaphore_wait(barrier, 4 * n_dp - 1 + n_dp * rows_met + ones_met)

    each(0, lambda j: xb_copy(j).start())
    each(1, lambda j: xf_copy(j).start())
    each(1, lambda j: gb_copy(j).start())

    lanes = lax.broadcasted_iota(jnp.int32, (tokens, 128), 1)
    rows8 = lax.broadcasted_iota(jnp.int32, (8, 128), 0)
    chunk = 512

    def statistics(ref):
        def lane_sum(fn):
            def step(c, acc):
                part = ref[:, pl.ds(pl.multiple_of(c * chunk, chunk), chunk)].astype(F32)
                part = fn(part)
                for i in range(chunk // 128):
                    acc = acc + part[:, i * 128 : (i + 1) * 128]
                return acc

            acc = lax.fori_loop(0, width // chunk, step, jnp.zeros((tokens, 128), F32))
            return jnp.sum(acc, axis=1, keepdims=True)

        mean = lane_sum(lambda v: v) / width

        def squared(v):
            return (v - mean) * (v - mean)

        rstd = lax.rsqrt(lane_sum(squared) / width + 1e-05)
        both = jnp.where(lanes == 0, mean, jnp.where(lanes == 1, rstd, 0.0))
        return both.T[0:8, :]

    s_load.wait()
    pb_own[...] = statistics(sv)
    each(0, lambda j: pb_copy(j).start())
    x_load.wait()
    own = statistics(xv)
    own = jnp.where(rows8 == 2, jnp.broadcast_to(fdoc_ref[...].astype(F32), (8, 128)), own)
    own = jnp.where(rows8 == 3, jnp.broadcast_to(bdoc_ref[...].astype(F32), (8, 128)), own)
    pf_own[...] = own
    pf[g] = own
    each(1, lambda j: pf_copy(j).start())

    row_ids = lax.broadcasted_iota(jnp.int32, (tokens, tokens), 0)
    col_ids = lax.broadcasted_iota(jnp.int32, (tokens, tokens), 1)
    causal = col_ids <= row_ids

    def wide(row):
        return jnp.broadcast_to(row, (128, 128)).T

    def allowed_of(docs):
        across = jnp.broadcast_to(docs, (128, 128))
        return causal & (across == across.T)

    ats = [slice(h * hd, (h + 1) * hd) for h in range(heads)]
    three = [slice(h * 3 * hd, (h + 1) * 3 * hd) for h in range(heads)]

    def projections(normed, at):
        projected = dot(normed, w_ref[at, : 3 * hd], NN)
        return (
            (projected[:, :hd] * scale).astype(BF16),
            projected[:, hd : 2 * hd].astype(BF16),
            projected[:, 2 * hd :].astype(BF16),
        )

    def probabilities(q, k, allowed):
        e = jnp.where(allowed, jnp.exp(dot(q, k, NT)), 0.0)
        return e * (1.0 / jnp.sum(e, axis=-1, keepdims=True))

    xf_load.wait()
    gb_load.wait()

    def forward(k, _):
        j = peer(k, -way)

        @pl.when(k > 0)
        def _():
            pf_in(j).wait_recv()
            xf_in(j).wait_recv()

        mean = wide(pf[j, 0:1, :])
        rstd = wide(pf[j, 1:2, :])
        allowed = allowed_of(pf[j, 2:3, :])
        qkv, probs, attended = [], [], []
        for at in ats:
            x = xf[j, :, at].astype(F32)
            normed = ((x - mean) * rstd * gain_ref[:, at].astype(F32)).astype(BF16)
            qkv.append(projections(normed, at))
        for q, key, v in qkv:
            probs.append(probabilities(q, key, allowed).astype(BF16))
        for p, (q, key, v) in zip(probs, qkv):
            attended.append(dot(p, v, NN).astype(BF16))
        for at, a in zip(ats, attended):
            x = xf[j, :, at].astype(F32)
            fwd_out[j, :, at] = (x + dot(a, w_ref[at, 3 * hd :], NT)).astype(BF16)
        aside = h_from & detour(j)

        @pl.when(aside)
        def _():
            ho_first(j).start()

        @pl.when(jnp.logical_not(aside))
        def _():
            ho_copy(j).start()

        return 0

    lax.fori_loop(0, n_dp, forward, 0)

    def park(k, _):
        j = peer(k, way)
        xb_copy(j).wait_send()

        @pl.when(k < ahead)
        def _():
            pa_copy(j).start()
        return 0

    lax.fori_loop(0, n_dp, park, 0)

    def early(k, _):
        j = peer(k, -way)

        @pl.when(k > 0)
        def _():
            gb_in(j).wait_recv()

        for at in ats:
            dab[j, :, at] = dot(gb[j, :, at], w_ref[at, 3 * hd :], NN).astype(BF16)
        return 0

    lax.fori_loop(0, n_dp, early, 0)
    dg[...] = jnp.zeros_like(dg)
    group_ids = lax.broadcasted_iota(jnp.int32, (n_dp, 128), 0)

    def backward(k, parts):
        j = peer(k, way)
        pb_in(j).wait_recv()
        xb_in(j).wait_recv()
        mean = wide(pb[j, 0:1, :])
        rstd = wide(pb[j, 1:2, :])
        allowed = allowed_of(pf[j, 3:4, :])
        qkv, probs, dscores = [], [], []
        for at in ats:
            gain = gain_ref[:, at].astype(F32)
            normed = ((xb[j, :, at].astype(F32) - mean) * rstd * gain).astype(BF16)
            nb[j, :, at] = normed
            qkv.append(projections(normed, at))
            vb[j, :, at] = qkv[-1][2]
        for at, (q, key, v) in zip(ats, qkv):
            probs.append(probabilities(q, key, allowed))
            pr[j, :, at] = probs[-1].astype(BF16)
        for h, at in enumerate(ats):
            p, p16, da = probs[h], probs[h].astype(BF16), dab[j, :, at]
            dp = dot(da, qkv[h][2], NT)
            dscores.append((p * (dp - jnp.sum(dp * p, axis=-1, keepdims=True))).astype(BF16))
            start = three[h].start
            dproj[j, :, start + 2 * hd : start + 3 * hd] = dot(p16, da, TN).astype(BF16)
        for h in range(heads):
            q, key, v = qkv[h]
            start = three[h].start
            dproj[j, :, start : start + hd] = (dot(dscores[h], key, NN) * scale).astype(BF16)
            dproj[j, :, start + hd : start + 2 * hd] = dot(dscores[h], q, TN).astype(BF16)
        first = jnp.zeros((tokens, hd), F32)
        second = jnp.zeros((tokens, hd), F32)
        for h, at in enumerate(ats):
            xhat = (xb[j, :, at].astype(F32) - mean) * rstd
            dn = dot(dproj[j, :, three[h]], w_ref[at, : 3 * hd], NT)
            dg[0:1, at] += jnp.sum(dn * xhat, axis=0, keepdims=True)
            back = dn * gain_ref[:, at].astype(F32)
            dxh[j, :, at] = back
            first = first + back
            second = second + back * xhat
        here = group_ids == j
        return (
            jnp.where(here, jnp.sum(first.T, axis=0, keepdims=True), parts[0]),
            jnp.where(here, jnp.sum(second.T, axis=0, keepdims=True), parts[1]),
        )

    blank = jnp.zeros((n_dp, 128), F32)
    parts = lax.fori_loop(0, n_dp, backward, (blank, blank))
    sums[g, 0] = parts[0]
    sums[g, 1] = parts[1]

    each(1, lambda j: su_copy(j).start())

    @pl.when(h_via)
    def _():
        forward_by(ho_second)

    each(1, lambda j: su_in(j).wait_recv())
    acc = sums[0]
    for i in range(1, n_dp):
        acc = acc + sums[i]
    total[...] = acc * (1.0 / width)

    @pl.when(s > 0)
    def _():
        def finish(k, _):
            j = peer(lax.rem(k + FIRST[n_dp], n_dp), way)
            mean = wide(pb[j, 0:1, :])
            rstd = wide(pb[j, 1:2, :])
            here = group_ids == j
            c1 = wide(jnp.sum(jnp.where(here, total[0], 0.0), axis=0, keepdims=True))
            c2 = wide(jnp.sum(jnp.where(here, total[1], 0.0), axis=0, keepdims=True))
            for h in range(heads):
                at = slice(h * hd, (h + 1) * hd)
                xhat = (xb[j, :, at].astype(F32) - mean) * rstd
                back = rstd * (dxh[j, :, at] - c1 - xhat * c2)
                bwd_out[j, :, at] = (gb[j, :, at].astype(F32) + back).astype(BF16)
            aside = r_from & detour(j)

            @pl.when(aside)
            def _():
                re_first(j).start()

            @pl.when(jnp.logical_not(aside))
            def _():
                re_copy(j).start()

            return 0

        lax.fori_loop(0, n_dp, finish, 0)

    @pl.when(r_via)
    def _():
        forward_by(re_second)

    def rest(k, _):
        pa_copy(peer(k, way)).start()
        return 0

    lax.fori_loop(ahead, n_dp, rest, 0)

    @pl.when(s == n_sec - 1)
    def _():
        zero[...] = jnp.zeros_like(zero)

        def fill(j):
            return pltpu.make_async_copy(zero, returned.at[:, span(j)], re_r.at[j])

        each(0, lambda j: fill(j).start())
        each(0, lambda j: fill(j).wait())

    def attend(j, _):
        for at in ats:
            ab[j, :, at] = dot(pr[j, :, at], vb[j, :, at], NN).astype(BF16)
        return 0

    lax.fori_loop(0, n_dp, attend, 0)
    every = n_dp * tokens
    for h, at in enumerate(ats):
        normed = nb[:, :, at].reshape(every, hd)
        into = dot(normed, dproj[:, :, three[h]].reshape(every, 3 * hd), TN)
        pgrad[at, : 3 * hd] = (into * (1.0 / n_dp)).astype(BF16)
        dy = gb[:, :, at].reshape(every, hd)
        out = dot(dy, ab[:, :, at].reshape(every, hd), TN)
        pgrad[at, 3 * hd :] = (out * (1.0 / n_dp)).astype(BF16)
    ggrad[...] = (dg[0:1, :] * (1.0 / n_dp)).astype(BF16)

    each(0, lambda j: ho_in(j).wait_recv())

    @pl.when(s < n_sec - 1)
    def _():
        each(0, lambda j: re_in(j).wait_recv())

    each(0, lambda j: pa_copy(j).wait_recv())
    @pl.when(h_via)
    def _():
        forwarded(ho_second)

    @pl.when(r_via)
    def _():
        forwarded(re_second)

    each(1, lambda j: xf_copy(j).wait_send())
    each(1, lambda j: gb_copy(j).wait_send())
    each(1, lambda j: pf_copy(j).wait_send())
    each(0, lambda j: pb_copy(j).wait_send())
    each(1, lambda j: su_copy(j).wait_send())
    each(0, lambda j: ho_copy(j).wait_send())

    @pl.when(s > 0)
    def _():
        each(0, lambda j: re_copy(j).wait_send())

    each(0, lambda j: pa_copy(j).wait_send())


def local(n_sec, n_dp, inputs, stash, grad_in, proj, gain, fwd_docs, bwd_docs):
    tokens, width = inputs.shape[1:]
    rows, four = proj.shape[1:]
    blocks = (n_dp, tokens, rows)
    row_sem = pltpu.SemaphoreType.DMA((n_dp,))
    anywhere = pl.BlockSpec(memory_space=pl.ANY)
    vmem = pl.BlockSpec(memory_space=pltpu.VMEM)
    handed, returned, parked, pgrad, ggrad = pl.pallas_call(
        functools.partial(kernel, n_sec, n_dp),
        out_shape=[jax.ShapeDtypeStruct((tokens, width), BF16)] * 3
        + [
            jax.ShapeDtypeStruct((rows, four), BF16),
            jax.ShapeDtypeStruct((1, rows), BF16),
        ],
        in_specs=[anywhere] * 3 + [vmem] * 4,
        out_specs=[anywhere] * 3 + [vmem] * 2,
        scratch_shapes=[
            pltpu.VMEM((tokens, width), BF16),
            pltpu.VMEM((tokens, width), BF16),
            pltpu.VMEM(blocks, BF16),
            pltpu.VMEM(blocks, BF16),
            pltpu.VMEM(blocks, BF16),
            pltpu.VMEM(blocks, BF16),
            pltpu.VMEM(blocks, BF16),
            pltpu.VMEM(blocks, F32),
            pltpu.VMEM(blocks, BF16),
            pltpu.VMEM(blocks, BF16),
            pltpu.VMEM(blocks, BF16),
            pltpu.VMEM(blocks, BF16),
            pltpu.VMEM(blocks, BF16),
            pltpu.VMEM((n_dp, tokens, 3 * rows), BF16),
            pltpu.VMEM((8, rows), F32),
            pltpu.VMEM((tokens, rows), BF16),
            pltpu.VMEM((8, 128), F32),
            pltpu.VMEM((8, 128), F32),
            pltpu.VMEM((n_dp, 8, 128), F32),
            pltpu.VMEM((n_dp, 8, 128), F32),
            pltpu.VMEM((n_dp, 2, n_dp, 128), F32),
            pltpu.VMEM((2, n_dp, 128), F32),
            pltpu.SemaphoreType.DMA((4,)),
        ]
        + [row_sem] * 20
        + [pltpu.VMEM(blocks, BF16)],
        compiler_params=pltpu.CompilerParams(
            collective_id=0, has_side_effects=True, vmem_limit_bytes=48 * 1024 * 1024
        ),
    )(inputs[0], stash[0], grad_in[0], proj[0], gain, fwd_docs, bwd_docs)
    return handed[None], returned[None], parked[None], pgrad[None], ggrad


def solution(mesh):
    n_sec, n_dp = mesh.shape["section"], mesh.shape["dp"]
    token_blocks = P("section", "dp", None)
    rows = P("section", "dp")
    return jax.shard_map(
        functools.partial(local, n_sec, n_dp),
        mesh=mesh,
        in_specs=(token_blocks,) * 4 + (rows,) * 3,
        out_specs=(token_blocks,) * 4 + (rows,),
        check_vma=False,
    )
```
